512 devices in a mesh: ctx: 128 (over x, z, core), ch: 4 (over y).
Axes of the slice: x: 4, y: 4, z: 16, core: 2. Of those that a mesh axis runs over, the one named last changes fastest.
Arguments:
- inputs_x: bfloat16 [16384, 2048], P('ctx', 'ch'), may hold values from -6 to 6
- grad_out: bfloat16 [16384, 2048], P('ctx', 'ch'), may hold values from -0.0625 to 0.0625
- filter_blocks: float32 [128, 128, 512], P('ctx'), may hold values from -12 to 12
- lag_block: int32 [128], replicated, may hold values from 0 to 127, each once
Outputs:
- grad_inputs: bfloat16 [16384, 2048], P('ctx', 'ch')
- grad_filter: float32 [128, 128, 512], P('ctx', None, 'ch')
The draws below stay inside these ranges and needn't reach their ends.
Inputs may be any that keep to these rules, and one draw needn't show every extreme that they name: Each value appears once: row q of filter_blocks holds lags lag_block[q] * 128 to lag_block[q] * 128 + 127.
All inputs are finite; a program needn't handle non-finite values.
Results may differ from the reference program's by a relative error of at most 0.001.
Values sent between devices are 32-bit elements; how exact they have to be, the bound alone decides.
A program may use at most 128 MiB of HBM per device.

```python
import jax
import jax.numpy as jnp

BLK = 128
CHANNELS = 2048
FILTERS = 512
TOKENS = 16384
N_CTX = 128
N_CH = 4


def levels(rng, shape, pieces, smallest, largest):
    loudness, own = 1.0, jax.random.fold_in(rng, 6)
    for position, blocks in pieces:
        heights = jnp.exp(jax.random.uniform(jax.random.fold_in(own, position), (blocks,), jnp.float32, smallest / len(pieces), largest / len(pieces)))
        loudness = loudness * jnp.repeat(heights, shape[position] // blocks).reshape([-1 if axis == position else 1 for axis in range(len(shape))])
    return loudness


def normal_values(rng, shape, deviation, reach, pieces=(), dtype=jnp.bfloat16):
    values = jax.random.normal(rng, shape, jnp.float32) * deviation
    if len(pieces) > 0:
        values = levels(rng, shape, pieces, -0.22, 0.18) * values
    return jnp.clip(values, min=-reach, max=reach).astype(dtype)


def setup_inputs(seed: int = 0) -> dict:
    keys = jax.random.split(jax.random.key(seed), 5)
    return {
        "inputs_x": normal_values(keys[0], (TOKENS, CHANNELS), 1.0, 6.0, ((0, 128), (1, 4))),
        "grad_out": normal_values(keys[1], (TOKENS, CHANNELS), (0.5 * TOKENS ** -0.5), 0.0625, ((0, 128), (1, 4))),
        "filter_blocks": normal_values(keys[2], (N_CTX, BLK, FILTERS), 2.0, 12.0, ((0, 128),), jnp.float32),
        "lag_block": jax.random.permutation(keys[3], N_CTX).astype(jnp.int32),
    }


def reference(inputs_x, grad_out, filter_blocks, lag_block):
    inverse_order = jnp.argsort(lag_block).astype(jnp.int32)
    filt_lags = filter_blocks[inverse_order].reshape(TOKENS, FILTERS).astype(jnp.float32)
    padded = 2 * TOKENS
    filt_spec = jnp.fft.rfft(filt_lags, n=padded, axis=0)
    grad_parts = []
    lag_total = jnp.zeros((TOKENS, FILTERS), jnp.float32)
    for group in range(N_CH):
        cot_slice = grad_out[:, group * FILTERS:(group + 1) * FILTERS].astype(jnp.float32)
        act_slice = inputs_x[:, group * FILTERS:(group + 1) * FILTERS].astype(jnp.float32)
        cot_spec = jnp.fft.rfft(cot_slice, n=padded, axis=0)
        act_spec = jnp.fft.rfft(act_slice, n=padded, axis=0)
        grad_rows = jnp.fft.irfft(cot_spec * jnp.conj(filt_spec), n=padded, axis=0)[:TOKENS]
        lag_rows = jnp.fft.irfft(cot_spec * jnp.conj(act_spec), n=padded, axis=0)[:TOKENS]
        grad_parts.append(grad_rows.astype(jnp.float32))
        lag_total = lag_total + lag_rows.astype(jnp.float32)
    grad_inputs = jnp.concatenate(grad_parts, axis=1).astype(jnp.bfloat16)
    grad_filter = lag_total.reshape(N_CTX, BLK, FILTERS)[lag_block]
    return grad_inputs, grad_filter
```

```python
import jax
import jax.numpy as jnp
from jax import lax
from jax.experimental import pallas as pl
from jax.experimental.pallas import tpu as pltpu
from jax.sharding import PartitionSpec as P

BF = jnp.bfloat16
F32 = jnp.float32

def conv_kernel(d_ref, x_ref, h_ref, lagcol_ref, lagrow_ref, g_ref, l_ref, dpad, xpad, hpad, hbank, xbank, w_ref, gacc, lacc):
    col = lax.broadcasted_iota(jnp.int32, (128, 128), 1)
    row = lax.broadcasted_iota(jnp.int32, (128, 128), 0)
    flip = (row + col == 127).astype(BF)
    take = (lagrow_ref[...] == row).astype(F32)
    h = jnp.dot(take, h_ref[...], precision=lax.Precision.HIGHEST, preferred_element_type=F32)
    hi = h.astype(BF)
    lo = (h - hi.astype(F32)).astype(BF)
    zeros = jnp.zeros((16, 128), F32)
    for part, val in enumerate((hi, lo)):
        hpad[part, pl.ds(0, 16), :] = zeros
        hpad[part, pl.ds(16, 128), :] = jnp.dot(val, flip, preferred_element_type=F32)
    for c in range(4):
        xpad[c, pl.ds(0, 16), :] = zeros
        xpad[c, pl.ds(16, 128), :] = jnp.dot(x_ref[c].astype(BF), flip, preferred_element_type=F32)
        dpad[c, pl.ds(0, 128), :] = d_ref[c]
        dpad[c, pl.ds(128, 8), :] = jnp.zeros((8, 128), F32)
    for r in range(16):
        lanes = pl.ds(r * 128, 128)
        for part in range(2):
            hbank[part, :, lanes] = hpad[part, pl.ds(r + 1, 128), :].astype(BF)
        for c in range(4):
            xbank[c, :, lanes] = xpad[c, pl.ds(r + 1, 128), :].astype(BF)
    gacc[...] = jnp.zeros_like(gacc)
    lacc[...] = jnp.zeros_like(lacc)
    late = col >= 127 - row
    for q in range(8):
        def build(r, _):
            for c in range(4):
                m = q * 16 + r
                now = jnp.broadcast_to(dpad[c, pl.ds(m, 1), :], (128, 128))
                nxt = jnp.broadcast_to(dpad[c, pl.ds(m + 1, 1), :], (128, 128))
                pick = jnp.where(late, now, nxt)
                w_ref[pl.ds(pl.multiple_of(r * 128, 128), 128), pl.ds(c * 128, 128)] = pltpu.roll(pick, 1, 1, stride=1, stride_axis=0).astype(BF)
            return 0
        lax.fori_loop(0, 16, build, 0)
        rows = 16 * (q + 1)
        out = pl.ds(128 - rows, rows)
        gacc[out, :] += jnp.dot(hbank[0, pl.ds(0, rows), :], w_ref[...], preferred_element_type=F32) + jnp.dot(hbank[1, pl.ds(0, rows), :], w_ref[...], preferred_element_type=F32)
        for c in range(4):
            lacc[out, :] += jnp.dot(xbank[c, pl.ds(0, rows), :], w_ref[:, pl.ds(c * 128, 128)], preferred_element_type=F32)
    for c in range(4):
        g_ref[c] = gacc[:, pl.ds(c * 128, 128)]
    put = (127 - lagcol_ref[...] == col).astype(F32)
    l_ref[...] = jnp.dot(put, lacc[...], precision=lax.Precision.HIGHEST, preferred_element_type=F32)

def conv(d, x, h, lag_block):
    v = pl.BlockSpec(memory_space=pltpu.VMEM)
    return pl.pallas_call(conv_kernel,
        out_shape=(jax.ShapeDtypeStruct((4, 128, 128), F32), jax.ShapeDtypeStruct((128, 128), F32)),
        in_specs=[v] * 5, out_specs=(v, v),
        scratch_shapes=[pltpu.VMEM((4, 136, 128), F32), pltpu.VMEM((4, 144, 128), F32), pltpu.VMEM((2, 144, 128), F32),
            pltpu.VMEM((2, 128, 2048), BF), pltpu.VMEM((4, 128, 2048), BF), pltpu.VMEM((2048, 512), BF),
            pltpu.VMEM((128, 512), F32), pltpu.VMEM((128, 128), F32)],
        compiler_params=pltpu.CompilerParams(vmem_limit_bytes=48 << 20),
    )(d, x, h, lag_block[:, None], lag_block[None, :])


def body(inputs_x, grad_out, filter_blocks, lag_block):
    both = jnp.stack([grad_out, inputs_x]).astype(F32)
    both = both.reshape(2, 128, 4, 128).transpose(3, 2, 0, 1)
    both = lax.all_to_all(both.reshape(512, 2, 128), ("ctx", "ch"), 0, 0, tiled=True)
    both = both.reshape(128, 4, 2, 128).transpose(2, 1, 0, 3)
    mine = lax.dynamic_slice_in_dim(filter_blocks[0], lax.axis_index("ch") * 128, 128, 1)
    rows = lax.all_to_all(mine.T, "ctx", 0, 0, tiled=True)
    g, l = conv(both[0], both[1], rows, lag_block)
    g = g[:, ::-1].transpose(1, 0, 2).reshape(512, 128)
    g = lax.all_to_all(g, ("ctx", "ch"), 0, 0, tiled=True)
    grad_inputs = g.reshape(128, 4, 128).transpose(2, 1, 0).reshape(128, 512).astype(BF)
    l = lax.all_to_all(l, "ctx", 0, 0, tiled=True)
    return grad_inputs, l.T[None]


def solution(mesh):
    in_specs = (P("ctx", "ch"), P("ctx", "ch"), P("ctx", None, None), P())
    out_specs = (P("ctx", "ch"), P("ctx", None, "ch"))
    return jax.shard_map(body, mesh=mesh, in_specs=in_specs, out_specs=out_specs, check_vma=False)
```

```python
import jax
import jax.numpy as jnp
from jax import lax
from jax.experimental import pallas as pl
from jax.experimental.pallas import tpu as pltpu
from jax.sharding import PartitionSpec as P

BF = jnp.bfloat16
F32 = jnp.float32
MESH = pl.DeviceIdType.MESH
N = 128
NZ = 16


def kernel(x_ref, d_ref, f_ref, lag_ref, gi_ref, gf_ref,
           own_d, own_x, y_dh, y_x, r_dh, r_x, gout, r_g, f_g, lout, r_l,
           dpad, xpad, hpad, hbank, xbank, w, lacc, send, recv, local):
    i = lax.axis_index("ctx")
    g = lax.axis_index("ch")
    px, pz, pc = lax.div(i, 2 * NZ), lax.rem(lax.div(i, 2), NZ), lax.rem(i, 2)

    def peer(k):
        k = N - 1 - k
        s = lax.div(k, 8)
        odd = lax.rem(s, 2)
        dz = odd * lax.div(s + 1, 2) + (1 - odd) * (NZ - lax.div(s, 2))
        z = lax.rem(pz + dz, NZ)
        x = lax.rem(px + lax.rem(lax.div(k, 2), 4), 4)
        return x * (2 * NZ) + z * 2 + lax.rem(pc + lax.rem(k, 2), 2)

    bar = pltpu.get_barrier_semaphore()

    def greet(k, _):
        pl.semaphore_signal(bar, inc=1, device_id=(peer(k), g), device_id_type=MESH)
        return 0

    lax.fori_loop(0, N - 1, greet, 0)
    for k in range(1, 4):
        pl.semaphore_signal(bar, inc=1, device_id=(i, lax.rem(g + k, 4)), device_id_type=MESH)

    for c in range(4):
        lanes = pl.ds(c * N, N)
        own_d[c] = d_ref[:, lanes].astype(F32).T
        own_x[c] = x_ref[:, lanes].astype(F32).T
    y_dh[4] = f_ref[:, pl.ds(pl.multiple_of(g * N, N), N)].T

    pl.semaphore_wait(bar, N + 2)

    def put(src, dst, n, device):
        pltpu.make_async_remote_copy(src_ref=src, dst_ref=dst, send_sem=send.at[n], recv_sem=recv.at[n],
                                     device_id=device, device_id_type=MESH).start()

    def keep(src, dst, n):
        copy = pltpu.make_async_copy(src, dst, local.at[n])
        copy.start()
        return copy

    def arrived(ref, n):
        pltpu.make_async_copy(ref, ref, recv.at[n]).wait()

    def sent(ref, n):
        pltpu.make_async_copy(ref, ref, send.at[n]).wait()

    def exchange_y(src, dst, n):
        for k in (2, 1, 3):
            to = lax.rem(g + k, 4)
            put(src.at[to], dst.at[g], n, (i, to))
        return keep(src.at[g], dst.at[g], n)

    def exchange_ctx(src, dst, n, row=lambda p: p):
        def go(k, _):
            p = peer(k)
            put(src.at[:, row(p), :], dst.at[:, i, :], n, (p, g))
            return 0

        lax.fori_loop(0, N - 1, go, 0)
        return keep(src.at[:, row(i), :], dst.at[:, i, :], n)

    most = pl.ds(0, N - 1)
    kept_d = exchange_y(own_d, y_dh, 0)
    kept_x = exchange_y(own_x, y_x, 1)
    kept_d.wait()
    arrived(own_d.at[pl.ds(0, 3)], 0)
    kept_dh = exchange_ctx(y_dh, r_dh, 2)
    kept_x.wait()
    arrived(own_x.at[pl.ds(0, 3)], 1)
    kept_rx = exchange_ctx(y_x, r_x, 3)

    kept_dh.wait()
    arrived(r_dh.at[:, most, :], 2)
    col = lax.broadcasted_iota(jnp.int32, (N, N), 1)
    row = lax.broadcasted_iota(jnp.int32, (N, N), 0)
    flip = (row + col == N - 1).astype(BF)
    lag = jnp.broadcast_to(lag_ref[...], (N, N))
    h = jnp.dot((lag == row).astype(F32), r_dh[4], precision=lax.Precision.HIGHEST, preferred_element_type=F32)
    hi = h.astype(BF)
    lo = (h - hi.astype(F32)).astype(BF)
    zeros = jnp.zeros((16, N), F32)
    for part, val in enumerate((hi, lo)):
        hpad[part, pl.ds(0, 16), :] = zeros
        hpad[part, pl.ds(16, N), :] = jnp.dot(val, flip, preferred_element_type=F32)
    for c in range(4):
        dpad[c, pl.ds(0, N), :] = r_dh[c]
        dpad[c, pl.ds(N, 8), :] = jnp.zeros((8, N), F32)
    for r in range(16):
        for part in range(2):
            hbank[part, :, pl.ds(r * N, N)] = hpad[part, pl.ds(r + 1, N), :].astype(BF)

    late = col >= N - 1 - row

    def build(m, _):
        for c in range(4):
            now = jnp.broadcast_to(dpad[c, pl.ds(m, 1), :], (N, N))
            nxt = jnp.broadcast_to(dpad[c, pl.ds(m + 1, 1), :], (N, N))
            pick = jnp.where(late, now, nxt)
            w[pl.ds(pl.multiple_of(m * N, N), N), pl.ds(c * N, N)] = pltpu.roll(pick, 1, 1, stride=1, stride_axis=0).astype(BF)
        return 0

    lax.fori_loop(0, N, build, 0, unroll=4)
    gout[...] = jnp.zeros_like(gout)
    for q in range(8):
        rows = 16 * (q + 1)
        part = jnp.dot(hbank[0, pl.ds(0, rows), :], w[pl.ds(q * 2048, 2048), :], preferred_element_type=F32)
        part += jnp.dot(hbank[1, pl.ds(0, rows), :], w[pl.ds(q * 2048, 2048), :], preferred_element_type=F32)
        for c in range(4):
            gout[c, pl.ds(N - rows, rows), :] += part[:, c * N:(c + 1) * N]
    kept_g = exchange_ctx(gout, r_g, 4, lambda p: N - 1 - p)

    kept_rx.wait()
    arrived(r_x.at[:, most, :], 3)
    for c in range(4):
        xpad[c, pl.ds(0, 16), :] = zeros
        xpad[c, pl.ds(16, N), :] = jnp.dot(r_x[c].astype(BF), flip, preferred_element_type=F32)
    for r in range(16):
        for c in range(4):
            xbank[c, :, pl.ds(r * N, N)] = xpad[c, pl.ds(r + 1, N), :].astype(BF)
    lacc[...] = jnp.zeros_like(lacc)
    for q in range(8):
        rows = 16 * (q + 1)
        part = jnp.zeros((rows, N), F32)
        for c in range(4):
            part += jnp.dot(xbank[c, pl.ds(0, rows), :], w[pl.ds(q * 2048, 2048), pl.ds(c * N, N)], preferred_element_type=F32)
        lacc[pl.ds(N - rows, rows), :] += part
    back = (N - 1 - lag == row).astype(F32).T
    lout[0] = jnp.dot(back, lacc[...], precision=lax.Precision.HIGHEST, preferred_element_type=F32)
    kept_l = exchange_ctx(lout, r_l, 5)

    kept_g.wait()
    arrived(r_g.at[:, most, :], 4)
    kept_f = exchange_y(r_g, f_g, 6)
    kept_l.wait()
    arrived(r_l.at[:, most, :], 5)
    gf_ref[...] = r_l[0].T
    kept_f.wait()
    arrived(r_g.at[pl.ds(0, 3)], 6)
    for c in range(4):
        gi_ref[:, pl.ds(c * N, N)] = f_g[c].T.astype(BF)

    sent(own_d.at[pl.ds(0, 3)], 0)
    sent(own_x.at[pl.ds(0, 3)], 1)
    sent(y_dh.at[:, most, :], 2)
    sent(y_x.at[:, most, :], 3)
    sent(gout.at[:, most, :], 4)
    sent(lout.at[:, most, :], 5)
    sent(r_g.at[pl.ds(0, 3)], 6)


def body(inputs_x, grad_out, filter_blocks, lag_block):
    v = pl.BlockSpec(memory_space=pltpu.VMEM)
    block = pltpu.VMEM((4, N, N), F32)
    gi, gf = pl.pallas_call(
        kernel,
        out_shape=(jax.ShapeDtypeStruct((N, 4 * N), BF), jax.ShapeDtypeStruct((N, N), F32)),
        in_specs=[v] * 4,
        out_specs=(v, v),
        scratch_shapes=[
            block, block, pltpu.VMEM((5, N, N), F32), block, pltpu.VMEM((5, N, N), F32), block, block, block, block,
            pltpu.VMEM((1, N, N), F32), pltpu.VMEM((1, N, N), F32),
            pltpu.VMEM((4, N + 8, N), F32), pltpu.VMEM((4, N + 16, N), F32), pltpu.VMEM((2, N + 16, N), F32),
            pltpu.VMEM((2, N, 16 * N), BF), pltpu.VMEM((4, N, 16 * N), BF), pltpu.VMEM((N * N, 4 * N), BF),
            pltpu.VMEM((N, N), F32),
            pltpu.SemaphoreType.DMA((7,)), pltpu.SemaphoreType.DMA((7,)), pltpu.SemaphoreType.DMA((7,)),
        ],
        compiler_params=pltpu.CompilerParams(collective_id=0, has_side_effects=True, vmem_limit_bytes=44 << 20),
    )(inputs_x, grad_out, filter_blocks[0], lag_block[None, :])
    return gi, gf[None]


def solution(mesh):
    in_specs = (P("ctx", "ch"), P("ctx", "ch"), P("ctx", None, None), P())
    out_specs = (P("ctx", "ch"), P("ctx", None, "ch"))
    return jax.shard_map(body, mesh=mesh, in_specs=in_specs, out_specs=out_specs, check_vma=False)
```

```python
import jax
import jax.numpy as jnp
from jax import lax
from jax.experimental import pallas as pl
from jax.experimental.pallas import tpu as pltpu
from jax.sharding import PartitionSpec as P

BF = jnp.bfloat16
F32 = jnp.float32
MESH = pl.DeviceIdType.MESH
N = 128
NZ = 16


def kernel(x_hbm, d_hbm, f_hbm, lag_hbm, gi_ref, gf_ref,
           x_in, d_in, f_in, lag_in, own_d, own_x, y_dh, y_x, r_dh, r_x, gout, r_g, f_g,
           dpad, xpad, hpad, hbank, xbank, w, lacc, send, recv, local):
    i = lax.axis_index("ctx")
    g = lax.axis_index("ch")
    px, pz, pc = lax.div(i, 2 * NZ), lax.rem(lax.div(i, 2), NZ), lax.rem(i, 2)
    around = [lax.rem(px + k, 4) * (2 * NZ) + lax.rem(pc + m, 2) for k in (0, 2, 1, 3) for m in (0, 1)]

    def each_peer(act):
        def at_distance(t, _):
            s = NZ - 1 - t
            odd = lax.rem(s, 2)
            dz = odd * lax.div(s + 1, 2) + (1 - odd) * (NZ - lax.div(s, 2))
            z = 2 * lax.rem(pz + dz, NZ)
            for a in around:
                act(a + z)
            return 0

        lax.fori_loop(0, NZ - 1, at_distance, 0)
        for a in around[1:]:
            act(a + 2 * pz)

    def keep(src, dst, n):
        copy = pltpu.make_async_copy(src, dst, local.at[n])
        copy.start()
        return copy

    def group(k):
        return lax.rem(g + k, 4)

    def lanes(k):
        return pl.ds(pl.multiple_of(group(k) * N, N), N)

    def greet(p):
        pl.semaphore_signal(bar, inc=1, device_id=(p, g), device_id_type=MESH)

    bar = pltpu.get_barrier_semaphore()
    for k in range(1, 4):
        pl.semaphore_signal(bar, inc=1, device_id=(i, group(k)), device_id_type=MESH)
    each_peer(greet)

    loads = [keep(d_hbm, d_in, 0), keep(f_hbm.at[0, :, lanes(0)], f_in, 1), keep(x_hbm, x_in, 2), keep(lag_hbm, lag_in, 3)]

    loads[0].wait()
    for k in range(1, 4):
        own_d[k - 1] = d_in[:, lanes(k)].astype(F32).T
    y_dh[1] = d_in[:, lanes(0)].astype(F32).T
    loads[1].wait()
    y_dh[0] = f_in[...].T
    loads[2].wait()
    for k in range(1, 4):
        own_x[k - 1] = x_in[:, lanes(k)].astype(F32).T
    y_x[0] = x_in[:, lanes(0)].astype(F32).T
    loads[3].wait()

    pl.semaphore_wait(bar, N + 2)

    def put(src, dst, n, device):
        pltpu.make_async_remote_copy(src_ref=src, dst_ref=dst, send_sem=send.at[n], recv_sem=recv.at[n],
                                     device_id=device, device_id_type=MESH).start()

    def arrived(ref, n):
        pltpu.make_async_copy(ref, ref, recv.at[n]).wait()

    def sent(ref, n):
        pltpu.make_async_copy(ref, ref, send.at[n]).wait()

    def exchange_ch(src, dst, n):
        for k in (2, 1, 3):
            put(src.at[k - 1], dst.at[3 - k], n, (i, group(k)))

    def exchange_ctx(src, dst, n, row=lambda p: p):
        each_peer(lambda p: put(src.at[:, row(p), :], dst.at[:, i, :], n, (p, g)))
        return keep(src.at[:, row(i), :], dst.at[:, i, :], n)

    most = pl.ds(0, N - 1)
    first, others = pl.ds(0, 2), pl.ds(2, 3)
    exchange_ch(own_d, y_dh.at[others], 0)
    exchange_ch(own_x, y_x.at[pl.ds(1, 3)], 1)
    kept_a = exchange_ctx(y_dh.at[first], r_dh.at[first], 4)
    arrived(own_d, 0)
    kept_b = exchange_ctx(y_dh.at[others], r_dh.at[others], 5)
    arrived(own_x, 1)
    kept_x = exchange_ctx(y_x, r_x, 6)

    col = lax.broadcasted_iota(jnp.int32, (N, N), 1)
    row = lax.broadcasted_iota(jnp.int32, (N, N), 0)
    flip = (row + col == N - 1).astype(BF)
    lag = jnp.broadcast_to(lag_in[...], (N, N))
    zeros = jnp.zeros((16, N), F32)
    late = col >= N - 1 - row

    def build(chans, unroll):
        for c in chans:
            dpad[c, pl.ds(0, N), :] = r_dh[c + 1]
            dpad[c, pl.ds(N, 8), :] = jnp.zeros((8, N), F32)

        def block(m, _):
            for c in chans:
                now = jnp.broadcast_to(dpad[c, pl.ds(m, 1), :], (N, N))
                nxt = jnp.broadcast_to(dpad[c, pl.ds(m + 1, 1), :], (N, N))
                pick = jnp.where(late, now, nxt)
                w[pl.ds(pl.multiple_of(m * N, N), N), pl.ds(c * N, N)] = pltpu.roll(pick, 1, 1, stride=1, stride_axis=0).astype(BF)
            return 0

        lax.fori_loop(0, N, block, 0, unroll=unroll)

    def grad_rows(c0, count, slot):
        for q in range(7, -1, -1):
            rows = 16 * (q + 1)
            part = jnp.dot(hbank[pl.ds(0, 2 * rows), :], w[pl.ds(q * 2048, 2048), pl.ds(c0 * N, count * N)], preferred_element_type=F32)
            part = part.reshape(q + 1, 2, 16, count * N)
            part = (part[:, 0] + part[:, 1]).reshape(rows, count * N)
            for c in range(count):
                if q == 7:
                    gout[slot + c] = part[:, c * N:(c + 1) * N]
                else:
                    gout[slot + c, pl.ds(N - rows, rows), :] += part[:, c * N:(c + 1) * N]

    kept_a.wait()
    arrived(r_dh.at[first, most, :], 4)
    h = jnp.dot((lag == row).astype(F32), r_dh[0], precision=lax.Precision.HIGHEST, preferred_element_type=F32)
    hi = h.astype(BF)
    lo = (h - hi.astype(F32)).astype(BF)
    for part, val in enumerate((hi, lo)):
        hpad[part, pl.ds(0, 16), :] = zeros
        hpad[part, pl.ds(16, N), :] = jnp.dot(val, flip, preferred_element_type=F32)
    for r in range(16):
        for part in range(2):
            val = hpad[part, pl.ds(r + 1, N), :].astype(BF)
            for t in range(8):
                hbank[pl.ds(32 * t + 16 * part, 16), pl.ds(r * N, N)] = val[16 * t:16 * t + 16]
    build((0,), 16)
    grad_rows(0, 1, 3)

    kept_b.wait()
    arrived(r_dh.at[others, most, :], 5)
    build((1, 2, 3), 4)
    grad_rows(1, 3, 0)
    early, last = pl.ds(0, 3), pl.ds(3, 2)
    kept_c = exchange_ctx(gout.at[early], r_g.at[early], 7, lambda p: N - 1 - p)

    kept_x.wait()
    arrived(r_x.at[:, most, :], 6)
    for c in range(4):
        xpad[c, pl.ds(0, 16), :] = zeros
        xpad[c, pl.ds(16, N), :] = jnp.dot(r_x[c].astype(BF), flip, preferred_element_type=F32)
    for r in range(16):
        for c in range(4):
            xbank[c, :, pl.ds(r * N, N)] = xpad[c, pl.ds(r + 1, N), :].astype(BF)
    for q in range(7, -1, -1):
        rows = 16 * (q + 1)
        part = jnp.zeros((rows, N), F32)
        for c in range(4):
            part += jnp.dot(xbank[c, pl.ds(0, rows), :], w[pl.ds(q * 2048, 2048), pl.ds(c * N, N)], preferred_element_type=F32)
        if q == 7:
            lacc[...] = part
        else:
            lacc[pl.ds(N - rows, rows), :] += part
    back = (N - 1 - lag == row).astype(BF)
    back = lax.dot_general(flip, back, (((1,), (1,)), ((), ())), preferred_element_type=F32)
    gout[4] = jnp.dot(back, lacc[...], precision=lax.Precision.HIGHEST, preferred_element_type=F32)
    kept_d = exchange_ctx(gout.at[last], r_g.at[last], 8, lambda p: N - 1 - p)

    kept_c.wait()
    arrived(r_g.at[early, most, :], 7)
    exchange_ch(r_g.at[early], f_g, 2)
    kept_d.wait()
    arrived(r_g.at[last, most, :], 8)
    gf_ref[...] = r_g[4].T
    gi_ref[:, lanes(0)] = r_g[3].T.astype(BF)
    arrived(f_g, 2)
    for k in range(1, 4):
        gi_ref[:, lanes(k)] = f_g[k - 1].T.astype(BF)

    sent(own_d, 0)
    sent(own_x, 1)
    sent(f_g, 2)
    sent(y_dh.at[first, most, :], 4)
    sent(y_dh.at[others, most, :], 5)
    sent(y_x.at[:, most, :], 6)
    sent(gout.at[early, most, :], 7)
    sent(gout.at[last, most, :], 8)


def body(inputs_x, grad_out, filter_blocks, lag_block):
    v = pl.BlockSpec(memory_space=pltpu.VMEM)

    def rows(n):
        return pltpu.VMEM((n, N, N), F32)

    gi, gf = pl.pallas_call(
        kernel,
        out_shape=(jax.ShapeDtypeStruct((N, 4 * N), BF), jax.ShapeDtypeStruct((N, N), F32)),
        in_specs=[pl.BlockSpec(memory_space=pltpu.HBM)] * 4,
        out_specs=(v, v),
        scratch_shapes=[
            pltpu.VMEM((N, 4 * N), BF), pltpu.VMEM((N, 4 * N), BF), pltpu.VMEM((N, N), F32), pltpu.VMEM((1, N), jnp.int32),
            rows(3), rows(3), rows(5), rows(4), rows(5), rows(4), rows(5), rows(5), rows(3),
            pltpu.VMEM((4, N + 8, N), F32), pltpu.VMEM((4, N + 16, N), F32), pltpu.VMEM((2, N + 16, N), F32),
            pltpu.VMEM((2 * N, 16 * N), BF), pltpu.VMEM((4, N, 16 * N), BF), pltpu.VMEM((N * N, 4 * N), BF),
            pltpu.VMEM((N, N), F32),
            pltpu.SemaphoreType.DMA((9,)), pltpu.SemaphoreType.DMA((9,)), pltpu.SemaphoreType.DMA((9,)),
        ],
        compiler_params=pltpu.CompilerParams(collective_id=0, has_side_effects=True, vmem_limit_bytes=56 << 20),
    )(inputs_x, grad_out, filter_blocks, lag_block[None, :])
    return gi, gf[None]


def solution(mesh):
    in_specs = (P("ctx", "ch"), P("ctx", "ch"), P("ctx", None, None), P())
    out_specs = (P("ctx", "ch"), P("ctx", None, "ch"))
    return jax.shard_map(body, mesh=mesh, in_specs=in_specs, out_specs=out_specs, check_vma=False)
```

```python
import jax
import jax.numpy as jnp
from jax import lax
from jax.experimental import pallas as pl
from jax.experimental.pallas import tpu as pltpu
from jax.sharding import PartitionSpec as P

BF = jnp.bfloat16
F32 = jnp.float32
MESH = pl.DeviceIdType.MESH
N = 128
NZ = 16


def kernel(x_hbm, d_hbm, f_hbm, lag_hbm, gi_ref, gf_ref,
           x_in, d_in, f_in, lag_in, own_d, own_x, y_dh, y_x, r_dh, r_x, gout, r_g, f_g,
           dpad, xpad, hpad, hbank, xbank, w, lacc, send, recv, local):
    i = lax.axis_index("ctx")
    g = lax.axis_index("ch")
    px, pz, pc = lax.div(i, 2 * NZ), lax.rem(lax.div(i, 2), NZ), lax.rem(i, 2)
    around = [lax.rem(px + k, 4) * (2 * NZ) + lax.rem(pc + m, 2) for k in (0, 2, 1, 3) for m in (0, 1)]

    def each_peer(act):
        def at_distance(t, _):
            s = NZ - 1 - t
            odd = lax.rem(s, 2)
            dz = odd * lax.div(s + 1, 2) + (1 - odd) * (NZ - lax.div(s, 2))
            z = 2 * lax.rem(pz + dz, NZ)
            for a in around:
                act(a + z)
            return 0

        lax.fori_loop(0, NZ - 1, at_distance, 0)
        for a in around[1:]:
            act(a + 2 * pz)

    def keep(src, dst, n):
        copy = pltpu.make_async_copy(src, dst, local.at[n])
        copy.start()
        return copy

    def group(k):
        return lax.rem(g + k, 4)

    def lanes(k):
        return pl.ds(pl.multiple_of(group(k) * N, N), N)

    def greet(p):
        pl.semaphore_signal(bar, inc=1, device_id=(p, g), device_id_type=MESH)

    bar = pltpu.get_barrier_semaphore()
    for k in range(1, 4):
        pl.semaphore_signal(bar, inc=1, device_id=(i, group(k)), device_id_type=MESH)
    each_peer(greet)

    loads = [keep(d_hbm, d_in, 0), keep(f_hbm.at[0, :, lanes(0)], f_in, 1), keep(x_hbm, x_in, 2), keep(lag_hbm, lag_in, 3)]

    loads[0].wait()
    for k in range(1, 4):
        own_d[k - 1] = d_in[:, lanes(k)].astype(F32).T
    y_dh[1] = d_in[:, lanes(0)].astype(F32).T
    loads[1].wait()
    y_dh[0] = f_in[...].T
    loads[2].wait()
    for k in range(1, 4):
        own_x[k - 1] = x_in[:, lanes(k)].astype(F32).T
    y_x[0] = x_in[:, lanes(0)].astype(F32).T
    loads[3].wait()

    pl.semaphore_wait(bar, N + 2)

    def put(src, dst, n, device):
        pltpu.make_async_remote_copy(src_ref=src, dst_ref=dst, send_sem=send.at[n], recv_sem=recv.at[n],
                                     device_id=device, device_id_type=MESH).start()

    def arrived(ref, n):
        pltpu.make_async_copy(ref, ref, recv.at[n]).wait()

    def sent(ref, n):
        pltpu.make_async_copy(ref, ref, send.at[n]).wait()

    def exchange_ch(src, dst, n):
        for k in (2, 1, 3):
            put(src.at[k - 1], dst.at[3 - k], n, (i, group(k)))

    def exchange_ctx(src, dst, n, row=lambda p: p):
        each_peer(lambda p: put(src.at[:, row(p), :], dst.at[:, i, :], n, (p, g)))
        return keep(src.at[:, row(i), :], dst.at[:, i, :], n)

    most = pl.ds(0, N - 1)
    first, others = pl.ds(0, 2), pl.ds(2, 3)
    exchange_ch(own_d, y_dh.at[others], 0)
    exchange_ch(own_x, y_x.at[pl.ds(1, 3)], 1)
    kept_a = exchange_ctx(y_dh.at[first], r_dh.at[first], 4)
    arrived(own_d, 0)
    kept_b = [exchange_ctx(y_dh.at[pl.ds(c + 1, 1)], r_dh.at[pl.ds(c + 1, 1)], 8 + c) for c in (1, 2, 3)]

    col = lax.broadcasted_iota(jnp.int32, (N, N), 1)
    row = lax.broadcasted_iota(jnp.int32, (N, N), 0)
    flip = (row + col == N - 1).astype(BF)
    lag = jnp.broadcast_to(lag_in[...], (N, N))
    zeros = jnp.zeros((16, N), F32)
    late = col >= N - 1 - row

    def build(chans, unroll):
        for c in chans:
            dpad[c, pl.ds(0, N), :] = r_dh[c + 1]
            dpad[c, pl.ds(N, 8), :] = jnp.zeros((8, N), F32)

        def block(m, _):
            for c in chans:
                now = jnp.broadcast_to(dpad[c, pl.ds(m, 1), :], (N, N))
                nxt = jnp.broadcast_to(dpad[c, pl.ds(m + 1, 1), :], (N, N))
                pick = jnp.where(late, now, nxt)
                w[pl.ds(pl.multiple_of(m * N, N), N), pl.ds(c * N, N)] = pltpu.roll(pick, 1, 1, stride=1, stride_axis=0).astype(BF)
            return 0

        lax.fori_loop(0, N, block, 0, unroll=unroll)

    def grad_rows(c0, count, slot):
        for q in range(7, -1, -1):
            rows = 16 * (q + 1)
            part = jnp.dot(hbank[pl.ds(0, 2 * rows), :], w[pl.ds(q * 2048, 2048), pl.ds(c0 * N, count * N)], preferred_element_type=F32)
            part = part.reshape(q + 1, 2, 16, count * N)
            part = (part[:, 0] + part[:, 1]).reshape(rows, count * N)
            for c in range(count):
                if q == 7:
                    gout[slot + c] = part[:, c * N:(c + 1) * N]
                else:
                    gout[slot + c, pl.ds(N - rows, rows), :] += part[:, c * N:(c + 1) * N]

    kept_a.wait()
    arrived(r_dh.at[first, most, :], 4)
    h = jnp.dot((lag == row).astype(F32), r_dh[0], precision=lax.Precision.HIGHEST, preferred_element_type=F32)
    hi = h.astype(BF)
    lo = (h - hi.astype(F32)).astype(BF)
    for part, val in enumerate((hi, lo)):
        hpad[part, pl.ds(0, 16), :] = zeros
        hpad[part, pl.ds(16, N), :] = jnp.dot(val, flip, preferred_element_type=F32)
    for r in range(16):
        for part in range(2):
            val = hpad[part, pl.ds(r + 1, N), :].astype(BF)
            for t in range(8):
                hbank[pl.ds(32 * t + 16 * part, 16), pl.ds(r * N, N)] = val[16 * t:16 * t + 16]
    build((0,), 16)

    for c in (1, 2, 3):
        kept_b[c - 1].wait()
        arrived(r_dh.at[pl.ds(c + 1, 1), most, :], 8 + c)
        if c == 1:
            arrived(own_x, 1)
            kept_x = exchange_ctx(y_x, r_x, 6)
        build((c,), 16)
    grad_rows(1, 3, 0)
    early, last = pl.ds(0, 3), pl.ds(3, 2)
    kept_c = exchange_ctx(gout.at[early], r_g.at[early], 7, lambda p: N - 1 - p)
    grad_rows(0, 1, 3)

    kept_x.wait()
    arrived(r_x.at[:, most, :], 6)
    for c in range(4):
        xpad[c, pl.ds(0, 16), :] = zeros
        xpad[c, pl.ds(16, N), :] = jnp.dot(r_x[c].astype(BF), flip, preferred_element_type=F32)
    for r in range(16):
        for c in range(4):
            xbank[c, :, pl.ds(r * N, N)] = xpad[c, pl.ds(r + 1, N), :].astype(BF)
    for q in range(7, -1, -1):
        rows = 16 * (q + 1)
        part = jnp.zeros((rows, N), F32)
        for c in range(4):
            part += jnp.dot(xbank[c, pl.ds(0, rows), :], w[pl.ds(q * 2048, 2048), pl.ds(c * N, N)], preferred_element_type=F32)
        if q == 7:
            lacc[...] = part
        else:
            lacc[pl.ds(N - rows, rows), :] += part
    back = (N - 1 - lag == row).astype(BF)
    back = lax.dot_general(flip, back, (((1,), (1,)), ((), ())), preferred_element_type=F32)
    gout[4] = jnp.dot(back, lacc[...], precision=lax.Precision.HIGHEST, preferred_element_type=F32)
    kept_d = exchange_ctx(gout.at[last], r_g.at[last], 8, lambda p: N - 1 - p)

    kept_c.wait()
    arrived(r_g.at[early, most, :], 7)
    exchange_ch(r_g.at[early], f_g, 2)
    kept_d.wait()
    arrived(r_g.at[last, most, :], 8)
    gf_ref[...] = r_g[4].T
    gi_ref[:, lanes(0)] = r_g[3].T.astype(BF)
    arrived(f_g, 2)
    for k in range(1, 4):
        gi_ref[:, lanes(k)] = f_g[k - 1].T.astype(BF)

    sent(own_d, 0)
    sent(own_x, 1)
    sent(f_g, 2)
    sent(y_dh.at[first, most, :], 4)
    for c in (1, 2, 3):
        sent(y_dh.at[pl.ds(c + 1, 1), most, :], 8 + c)
    sent(y_x.at[:, most, :], 6)
    sent(gout.at[early, most, :], 7)
    sent(gout.at[last, most, :], 8)


def body(inputs_x, grad_out, filter_blocks, lag_block):
    v = pl.BlockSpec(memory_space=pltpu.VMEM)

    def rows(n):
        return pltpu.VMEM((n, N, N), F32)

    gi, gf = pl.pallas_call(
        kernel,
        out_shape=(jax.ShapeDtypeStruct((N, 4 * N), BF), jax.ShapeDtypeStruct((N, N), F32)),
        in_specs=[pl.BlockSpec(memory_space=pltpu.HBM)] * 4,
        out_specs=(v, v),
        scratch_shapes=[
            pltpu.VMEM((N, 4 * N), BF), pltpu.VMEM((N, 4 * N), BF), pltpu.VMEM((N, N), F32), pltpu.VMEM((1, N), jnp.int32),
            rows(3), rows(3), rows(5), rows(4), rows(5), rows(4), rows(5), rows(5), rows(3),
            pltpu.VMEM((4, N + 8, N), F32), pltpu.VMEM((4, N + 16, N), F32), pltpu.VMEM((2, N + 16, N), F32),
            pltpu.VMEM((2 * N, 16 * N), BF), pltpu.VMEM((4, N, 16 * N), BF), pltpu.VMEM((N * N, 4 * N), BF),
            pltpu.VMEM((N, N), F32),
            pltpu.SemaphoreType.DMA((12,)), pltpu.SemaphoreType.DMA((12,)), pltpu.SemaphoreType.DMA((12,)),
        ],
        compiler_params=pltpu.CompilerParams(collective_id=0, has_side_effects=True, vmem_limit_bytes=int(53.65 * 2**20)),
    )(inputs_x, grad_out, filter_blocks, lag_block[None, :])
    return gi, gf[None]


def solution(mesh):
    in_specs = (P("ctx", "ch"), P("ctx", "ch"), P("ctx", None, None), P())
    out_specs = (P("ctx", "ch"), P("ctx", None, "ch"))
    return jax.shard_map(body, mesh=mesh, in_specs=in_specs, out_specs=out_specs, check_vma=False)
```

```python
import jax
import jax.numpy as jnp
from jax import lax
from jax.experimental import pallas as pl
from jax.experimental.pallas import tpu as pltpu
from jax.sharding import PartitionSpec as P

BF = jnp.bfloat16
F32 = jnp.float32
MESH = pl.DeviceIdType.MESH
N = 128
NZ = 16


def kernel(x_hbm, d_hbm, f_hbm, lag_hbm, gi_ref, gf_ref,
           x_in, d_in, f_in, lag_in, own_d, own_x, y_dh, y_x, r_dh, r_x, gout, r_g, f_g,
           dpad, xpad, hpad, hbank, xbank, w, lacc, send, recv, local):
    i = lax.axis_index("ctx")
    g = lax.axis_index("ch")
    px, pz, pc = lax.div(i, 2 * NZ), lax.rem(lax.div(i, 2), NZ), lax.rem(i, 2)
    around = [lax.rem(px + k, 4) * (2 * NZ) + lax.rem(pc + m, 2) for k in (0, 2, 1, 3) for m in (0, 1)]

    def each_peer(act):
        def at_distance(t, _):
            s = NZ - 1 - t
            odd = lax.rem(s, 2)
            dz = odd * lax.div(s + 1, 2) + (1 - odd) * (NZ - lax.div(s, 2))
            z = 2 * lax.rem(pz + dz, NZ)
            for a in around:
                act(a + z)
            return 0

        lax.fori_loop(0, NZ - 1, at_distance, 0)
        for a in around[1:]:
            act(a + 2 * pz)

    def keep(src, dst, n):
        copy = pltpu.make_async_copy(src, dst, local.at[n])
        copy.start()
        return copy

    def group(k):
        return lax.rem(g + k, 4)

    def lanes(k):
        return pl.ds(pl.multiple_of(group(k) * N, N), N)

    def greet(p):
        pl.semaphore_signal(bar, inc=1, device_id=(p, g), device_id_type=MESH)

    loads = [keep(d_hbm, d_in, 0), keep(f_hbm.at[0, :, lanes(0)], f_in, 1), keep(x_hbm, x_in, 2), keep(lag_hbm, lag_in, 3)]
    bar = pltpu.get_barrier_semaphore()
    for k in range(1, 4):
        pl.semaphore_signal(bar, inc=1, device_id=(i, group(k)), device_id_type=MESH)
    each_peer(greet)

    loads[0].wait()
    for k in range(1, 4):
        own_d[k - 1] = d_in[:, lanes(k)].astype(F32).T
    y_dh[1] = d_in[:, lanes(0)].astype(F32).T
    loads[1].wait()
    y_dh[0] = f_in[...].T

    pl.semaphore_wait(bar, N + 2)

    def put(src, dst, n, device):
        pltpu.make_async_remote_copy(src_ref=src, dst_ref=dst, send_sem=send.at[n], recv_sem=recv.at[n],
                                     device_id=device, device_id_type=MESH).start()

    def arrived(ref, n):
        pltpu.make_async_copy(ref, ref, recv.at[n]).wait()

    def sent(ref, n):
        pltpu.make_async_copy(ref, ref, send.at[n]).wait()

    def exchange_ch(src, dst, n):
        for k in (2, 1, 3):
            put(src.at[k - 1], dst.at[3 - k], n, (i, group(k)))

    def exchange_ctx(src, dst, n, row=lambda p: p):
        each_peer(lambda p: put(src.at[:, row(p), :], dst.at[:, i, :], n, (p, g)))
        return keep(src.at[:, row(i), :], dst.at[:, i, :], n)

    most = pl.ds(0, N - 1)
    first, others = pl.ds(0, 2), pl.ds(2, 3)
    exchange_ch(own_d, y_dh.at[others], 0)
    kept_a = exchange_ctx(y_dh.at[first], r_dh.at[first], 4)
    loads[2].wait()
    for k in range(1, 4):
        own_x[k - 1] = x_in[:, lanes(k)].astype(F32).T
    y_x[0] = x_in[:, lanes(0)].astype(F32).T
    loads[3].wait()
    exchange_ch(own_x, y_x.at[pl.ds(1, 3)], 1)
    arrived(own_d, 0)
    kept_b = [exchange_ctx(y_dh.at[pl.ds(c + 1, 1)], r_dh.at[pl.ds(c + 1, 1)], 8 + c) for c in (1, 2, 3)]

    col = lax.broadcasted_iota(jnp.int32, (N, N), 1)
    row = lax.broadcasted_iota(jnp.int32, (N, N), 0)
    flip = (row + col == N - 1).astype(BF)
    lag = jnp.broadcast_to(lag_in[...], (N, N))
    zeros = jnp.zeros((16, N), F32)
    late = col >= N - 1 - row

    def build(chans, unroll):
        for c in chans:
            dpad[c, pl.ds(0, N), :] = r_dh[c + 1]
            dpad[c, pl.ds(N, 8), :] = jnp.zeros((8, N), F32)

        def block(m, _):
            for c in chans:
                now = jnp.broadcast_to(dpad[c, pl.ds(m, 1), :], (N, N))
                nxt = jnp.broadcast_to(dpad[c, pl.ds(m + 1, 1), :], (N, N))
                pick = jnp.where(late, now, nxt)
                w[pl.ds(pl.multiple_of(m * N, N), N), pl.ds(c * N, N)] = pltpu.roll(pick, 1, 1, stride=1, stride_axis=0).astype(BF)
            return 0

        lax.fori_loop(0, N, block, 0, unroll=unroll)

    def grad_rows(c0, count, slot):
        for q in range(7, -1, -1):
            rows = 16 * (q + 1)
            part = jnp.dot(hbank[pl.ds(0, 2 * rows), :], w[pl.ds(q * 2048, 2048), pl.ds(c0 * N, count * N)], preferred_element_type=F32)
            part = part.reshape(q + 1, 2, 16, count * N)
            part = (part[:, 0] + part[:, 1]).reshape(rows, count * N)
            for c in range(count):
                if q == 7:
                    gout[slot + c] = part[:, c * N:(c + 1) * N]
                else:
                    gout[slot + c, pl.ds(N - rows, rows), :] += part[:, c * N:(c + 1) * N]

    kept_a.wait()
    arrived(r_dh.at[first, most, :], 4)
    h = jnp.dot((lag == row).astype(F32), r_dh[0], precision=lax.Precision.HIGHEST, preferred_element_type=F32)
    hi = h.astype(BF)
    lo = (h - hi.astype(F32)).astype(BF)
    for part, val in enumerate((hi, lo)):
        hpad[part, pl.ds(0, 16), :] = zeros
        hpad[part, pl.ds(16, N), :] = jnp.dot(val, flip, preferred_element_type=F32)
    for r in range(16):
        for part in range(2):
            val = hpad[part, pl.ds(r + 1, N), :].astype(BF)
            for t in range(8):
                hbank[pl.ds(32 * t + 16 * part, 16), pl.ds(r * N, N)] = val[16 * t:16 * t + 16]
    build((0,), 16)

    for c in (1, 2, 3):
        kept_b[c - 1].wait()
        arrived(r_dh.at[pl.ds(c + 1, 1), most, :], 8 + c)
        if c == 1:
            arrived(own_x, 1)
            kept_x = exchange_ctx(y_x, r_x, 6)
        build((c,), 16)
    grad_rows(1, 3, 0)
    early, last = pl.ds(0, 3), pl.ds(3, 2)
    kept_c = exchange_ctx(gout.at[early], r_g.at[early], 7, lambda p: N - 1 - p)
    grad_rows(0, 1, 3)

    kept_x.wait()
    arrived(r_x.at[:, most, :], 6)
    for c in range(4):
        xpad[c, pl.ds(0, 16), :] = zeros
        xpad[c, pl.ds(16, N), :] = jnp.dot(r_x[c].astype(BF), flip, preferred_element_type=F32)
    for r in range(16):
        for c in range(4):
            xbank[c, :, pl.ds(r * N, N)] = xpad[c, pl.ds(r + 1, N), :].astype(BF)
    for q in range(7, -1, -1):
        rows = 16 * (q + 1)
        part = jnp.zeros((rows, N), F32)
        for c in range(4):
            part += jnp.dot(xbank[c, pl.ds(0, rows), :], w[pl.ds(q * 2048, 2048), pl.ds(c * N, N)], preferred_element_type=F32)
        if q == 7:
            lacc[...] = part
        else:
            lacc[pl.ds(N - rows, rows), :] += part
    back = (N - 1 - lag == row).astype(BF)
    back = lax.dot_general(flip, back, (((1,), (1,)), ((), ())), preferred_element_type=F32)
    gout[4] = jnp.dot(back, lacc[...], precision=lax.Precision.HIGHEST, preferred_element_type=F32)
    kept_d = exchange_ctx(gout.at[last], r_g.at[last], 8, lambda p: N - 1 - p)

    kept_c.wait()
    arrived(r_g.at[early, most, :], 7)
    exchange_ch(r_g.at[early], f_g, 2)
    kept_d.wait()
    arrived(r_g.at[last, most, :], 8)
    gf_ref[...] = r_g[4].T
    gi_ref[:, lanes(0)] = r_g[3].T.astype(BF)
    arrived(f_g, 2)
    for k in range(1, 4):
        gi_ref[:, lanes(k)] = f_g[k - 1].T.astype(BF)

    sent(own_d, 0)
    sent(own_x, 1)
    sent(f_g, 2)
    sent(y_dh.at[first, most, :], 4)
    for c in (1, 2, 3):
        sent(y_dh.at[pl.ds(c + 1, 1), most, :], 8 + c)
    sent(y_x.at[:, most, :], 6)
    sent(gout.at[early, most, :], 7)
    sent(gout.at[last, most, :], 8)


def body(inputs_x, grad_out, filter_blocks, lag_block):
    v = pl.BlockSpec(memory_space=pltpu.VMEM)

    def rows(n):
        return pltpu.VMEM((n, N, N), F32)

    gi, gf = pl.pallas_call(
        kernel,
        out_shape=(jax.ShapeDtypeStruct((N, 4 * N), BF), jax.ShapeDtypeStruct((N, N), F32)),
        in_specs=[pl.BlockSpec(memory_space=pltpu.HBM)] * 4,
        out_specs=(v, v),
        scratch_shapes=[
            pltpu.VMEM((N, 4 * N), BF), pltpu.VMEM((N, 4 * N), BF), pltpu.VMEM((N, N), F32), pltpu.VMEM((1, N), jnp.int32),
            rows(3), rows(3), rows(5), rows(4), rows(5), rows(4), rows(5), rows(5), rows(3),
            pltpu.VMEM((4, N + 8, N), F32), pltpu.VMEM((4, N + 16, N), F32), pltpu.VMEM((2, N + 16, N), F32),
            pltpu.VMEM((2 * N, 16 * N), BF), pltpu.VMEM((4, N, 16 * N), BF), pltpu.VMEM((N * N, 4 * N), BF),
            pltpu.VMEM((N, N), F32),
            pltpu.SemaphoreType.DMA((12,)), pltpu.SemaphoreType.DMA((12,)), pltpu.SemaphoreType.DMA((12,)),
        ],
        compiler_params=pltpu.CompilerParams(collective_id=0, has_side_effects=True, vmem_limit_bytes=int(53.65 * 2**20)),
    )(inputs_x, grad_out, filter_blocks, lag_block[None, :])
    return gi, gf[None]


def solution(mesh):
    in_specs = (P("ctx", "ch"), P("ctx", "ch"), P("ctx", None, None), P())
    out_specs = (P("ctx", "ch"), P("ctx", None, "ch"))
    return jax.shard_map(body, mesh=mesh, in_specs=in_specs, out_specs=out_specs, check_vma=False)
```
